1024 devices in a mesh: section: 16 (over z_hi, x), st: 16 (over y, core), dp: 4 (over z_lo).
Axes of the slice: x: 4, y: 8, z: 16 (z_hi: 4, z_lo: 4; z = z_hi * 4 + z_lo), core: 2. Of those that a mesh axis runs over, the one named last changes fastest.
Arguments:
- saved_qkv: bfloat16 [16, 4, 3, 128, 48, 128], P('section', 'dp', None, None, 'st'), may hold values from -9 to 9
- positions: int32 [16, 4, 128], P('section', 'dp'), may hold values from 0 to 127, as said below
- w_out: bfloat16 [16, 6144, 6144], P('section', None, 'st'), may hold values from -0.078125 to 0.078125
- grad_out: bfloat16 [16, 4, 128, 6144], P('section', 'dp', None, 'st'), may hold values from -6 to 6
Outputs:
- grad_weight: bfloat16 [16, 6144, 6144], P('section', 'dp', 'st')
- upstream: bfloat16 [16, 4, 3, 128, 48, 128], P('section', 'dp', None, None, 'st')
The draws below stay inside these ranges and needn't reach their ends.
Inputs may be any that keep to these rules, and one draw needn't show every extreme that they name: `positions`: each row holds every number 0 to 127 once.
All inputs are finite; a program needn't handle non-finite values.
Results may differ from the reference program's by a relative error of at most 0.0095.
Values may be sent and summed in bfloat16 or wider, within the bound.
A program may use at most 32 MiB of HBM per device.

```python
import math
import jax
import jax.numpy as jnp
from jax import lax

D = 6144
HEADS = 48
DH = 128
SEQ = 128
SECTIONS = 16
REPLICAS = 4


def order_tables(key):
    row_count = SECTIONS * REPLICAS
    row_keys = jax.random.split(jax.random.fold_in(key, 17), row_count)
    permuted = jax.vmap(lambda single: jax.random.permutation(single, SEQ))(row_keys)
    return permuted.reshape(SECTIONS, REPLICAS, SEQ).astype(jnp.int32)


def draw_positions(key, part):
    return order_tables(key)


def draw_saved_qkv(key, part):
    dims_all = (SECTIONS, REPLICAS, 3, SEQ, HEADS, DH)
    base_key = jax.random.fold_in(key, 29)
    return jnp.clip(jax.random.normal(base_key, dims_all, jnp.float32), -4.0, 4.0).astype(jnp.bfloat16)


def spiked(values, rng, source, target, parts, factor):
    def block_of(dim):
        return (jnp.arange(values.shape[dim]) // (values.shape[dim] // parts)).reshape((-1,) + (1,) * (values.ndim - 1 - dim))

    near = jax.random.permutation(rng, parts)[block_of(target)]
    other_side = (block_of(target) + parts // 2) % parts
    return jnp.where((block_of(source) == near) | (block_of(source) == other_side), factor * values, values)


def block_levels(stream_key, shape, shards, low, high):
    def one(position, shards_of):
        heights = jax.random.uniform(jax.random.fold_in(jax.random.fold_in(stream_key, 6), position), (shards_of,), jnp.float32, low / len(shards), high / len(shards))
        return jnp.repeat(jnp.exp(heights), shape[position] // shards_of).reshape((-1,) + (1,) * (len(shape) - position - 1))

    loudness = one(*shards[0])
    for cut in shards[1:]:
        loudness = loudness * one(*cut)
    return loudness


def bell_draw(own_key, dims, scale, bound, cuts=(), held_as=jnp.bfloat16):
    result = scale * jax.random.normal(own_key, dims, jnp.float32)
    if cuts:
        result = result * block_levels(own_key, dims, cuts, -0.22, 0.18)
    return jnp.clip(result, -bound, bound).astype(held_as)


def gaussian_with(rng, dims, deviation, bound, cuts, heavy, dtype=jnp.bfloat16):
    drawn = deviation * jax.random.normal(rng, dims, jnp.float32)
    if cuts:
        drawn = drawn * block_levels(rng, dims, cuts, -0.22, 0.18)
    return jnp.clip(spiked(drawn, jax.random.fold_in(rng, 3), *heavy), -bound, bound).astype(dtype)


def setup_inputs(seed: int = 0) -> dict:
    splits = jax.random.split(jax.random.key(seed), 5)
    saved_qkv = draw_saved_qkv(jax.random.fold_in(splits[4], 71), 0)
    positions = draw_positions(jax.random.fold_in(splits[4], 71), 0)
    w_out = bell_draw(splits[2], (SECTIONS, D, HEADS * DH), (HEADS * DH) ** -0.5, 0.078125, ((0, 16), (2, 16)))
    grad_out = gaussian_with(splits[3], (SECTIONS, REPLICAS, SEQ, D), 1.0, 6.0, ((0, 16), (1, 4), (3, 16)), (1, 3, 4, 2.0))
    return dict(saved_qkv=saved_qkv, positions=positions, w_out=w_out, grad_out=grad_out)


def attend_backward(qkv_rows, token_pos, w_section, grad_rows):
    inv_root = 1.0 / math.sqrt(qkv_rows.shape[-1])
    queries = qkv_rows[0].astype(jnp.float32)
    key_rows = qkv_rows[1].astype(jnp.float32)
    values = qkv_rows[2].astype(jnp.float32)
    scores = jnp.einsum('qhd,khd->hqk', queries, key_rows) * inv_root
    visible = token_pos[None, :] <= token_pos[:, None]
    scores = jnp.where(visible[None], scores, -1e+30)
    highest = lax.optimization_barrier(jnp.max(scores, axis=2, keepdims=True))
    exponent = jnp.exp(scores - highest)
    softmax_out = exponent / lax.optimization_barrier(jnp.sum(exponent, axis=2, keepdims=True))
    weights_bf = softmax_out.astype(jnp.bfloat16)
    attended = jnp.einsum('hqk,khd->qhd', weights_bf.astype(jnp.float32), values).astype(jnp.bfloat16)
    seq_len = attended.shape[0]
    flat_att = attended.reshape(seq_len, -1)
    d_flat = jnp.dot(grad_rows, w_section, preferred_element_type=jnp.float32).astype(jnp.bfloat16)
    d_heads = d_flat.reshape(attended.shape).astype(jnp.float32)
    d_values = jnp.einsum('hqk,qhd->khd', weights_bf.astype(jnp.float32), d_heads).astype(jnp.bfloat16)
    d_weights = jnp.einsum('qhd,khd->hqk', d_heads, values)
    row_dot = lax.optimization_barrier(jnp.sum(softmax_out * d_weights, axis=2, keepdims=True))
    d_scores = (softmax_out * (d_weights - row_dot)).astype(jnp.bfloat16).astype(jnp.float32)
    d_queries = (jnp.einsum('hqk,khd->qhd', d_scores, key_rows) * inv_root).astype(jnp.bfloat16)
    d_keys = (jnp.einsum('hqk,qhd->khd', d_scores, queries) * inv_root).astype(jnp.bfloat16)
    return (flat_att, jnp.stack([d_queries, d_keys, d_values]))

def reference(saved_qkv, positions, w_out, grad_out):

    def per_section(section_items):
        qkv_section, pos_section, w_section, grad_section = section_items

        def per_replica(running, replica_items):
            qkv_rows, token_pos, grad_rows = replica_items
            flat_att, grad_qkv = attend_backward(qkv_rows, token_pos, w_section, grad_rows)
            partial_term = jnp.dot(grad_rows.T, flat_att, preferred_element_type=jnp.float32)
            rounded = lax.optimization_barrier(partial_term.astype(jnp.bfloat16))
            return (running + rounded.astype(jnp.float32), grad_qkv)
        start_sum = jnp.zeros((w_section.shape[0], w_section.shape[1]), jnp.float32)
        running, grad_all = lax.scan(per_replica, start_sum, (qkv_section, pos_section, grad_section))
        return (running.astype(jnp.bfloat16), grad_all)
    grad_weight, grad_all = lax.map(per_section, (saved_qkv, positions, w_out, grad_out))
    upstream = jnp.concatenate([grad_all[1:], jnp.zeros_like(grad_all[:1])], axis=0)
    return (grad_weight, upstream)
```

```python
import math

import jax
import jax.numpy as jnp
from jax import lax
from jax.experimental import pallas as pl
from jax.experimental.pallas import tpu as pltpu
from jax.sharding import PartitionSpec as P

MESH = pl.DeviceIdType.MESH
F32, BF16 = jnp.float32, jnp.bfloat16
SEQ, DH, NH, COLS = 128, 128, 3, 384
HALF = SEQ // 2
VMEM_LIMIT = 56 * 2**20


def dot(a, b, ca, cb):
    return lax.dot_general(a, b, (((ca,), (cb,)), ((), ())), preferred_element_type=F32)


def probs_t(qkv, pos, h):
    scores = dot(qkv[NH + h], qkv[h], 1, 1) * (1.0 / math.sqrt(DH))
    pos_q = jnp.broadcast_to(pos[...], (SEQ, SEQ))
    scores = jnp.where(pos_q.T <= pos_q, scores, -1e30)
    e = jnp.exp(scores - jnp.max(scores, axis=0, keepdims=True))
    return e / jnp.sum(e, axis=0, keepdims=True)


def kernel(
    qkv_in, pos_in, w_in, grad_in, dw_out, up_out,
    gath, w_v, qkv_o, pos_o, qkv_u, pos_u, relay, relay2, att, gd, acc, d_own, d_up, p_up,
    loc, g_s, g_r, b_s, b_r, z_s, z_r, a_s, a_r, e_s, e_r, l_s, l_r, x_s, x_r,
):
    s, t, d = lax.axis_index("section"), lax.axis_index("st"), lax.axis_index("dp")
    y, c = t // 2, t % 2
    x, hi = s % 4, s // 4
    base = hi * 4
    sib = y * 2 + 1 - c
    crosses = hi > 0

    def row(j, core=None):
        return lax.rem(y + 8 + j, 8) * 2 + (c if core is None else core)

    def remote(src, dst, ss, rs, dev):
        return pltpu.make_async_remote_copy(
            src_ref=src, dst_ref=dst, send_sem=ss, recv_sem=rs, device_id=dev, device_id_type=MESH
        )

    bar = pltpu.get_barrier_semaphore()

    def greet(dev):
        pl.semaphore_signal(bar, inc=1, device_id=dev, device_id_type=MESH)

    for j in (1, -1, 2, -2):
        greet((s, row(j), d))
    greet((s, sib, d))
    for i in (1, 2, 3):
        greet((s, t, lax.rem(d + i, 4)))
        greet((base + lax.rem(x + i, 4), t, d))

    @pl.when(jnp.logical_and(x == 3, hi < 3))
    def _():
        for i in range(4):
            greet((base + 4 + i, t, d))

    locals_ = [
        pltpu.make_async_copy(qkv_in, qkv_o, loc.at[0]),
        pltpu.make_async_copy(pos_in, pos_o, loc.at[1]),
        pltpu.make_async_copy(grad_in, gath.at[t], loc.at[2]),
        pltpu.make_async_copy(w_in, w_v, loc.at[3]),
    ]
    for copy in locals_:
        copy.start()

    pl.semaphore_wait(bar, 11 + jnp.where(crosses, 1, 0))

    lo, up = pl.ds(0, HALF), pl.ds(HALF, HALF)

    def own(j, rows, i):
        return remote(grad_in.at[rows], gath.at[t, rows], g_s.at[i], g_r.at[i], (s, row(j), d))

    def onward(start, j, rows, i):
        k = row(start)
        return remote(gath.at[k, rows], gath.at[k, rows], g_s.at[i], g_r.at[i], (s, row(j), d))

    p2 = [own(2, lo, 0), own(2, up, 1)]
    m2 = [own(-2, lo, 2), own(-2, up, 3)]
    p1, m1 = own(1, pl.ds(0, SEQ), 4), own(-1, pl.ds(0, SEQ), 5)
    p3 = [onward(-2, 1, lo, 6), onward(-2, 1, up, 7)]
    m3 = [onward(2, -1, lo, 8), onward(2, -1, up, 9)]
    p4, m4 = onward(-2, 2, lo, 10), onward(2, -2, up, 11)

    p2[0].start()
    m2[1].start()
    p2[1].start()
    m2[0].start()
    p1.start()
    m1.start()

    def beside(j, i):
        k = row(j)
        return remote(gath.at[k], gath.at[k], b_s.at[i], b_r.at[i], (s, sib, d))

    ring = (0, 1, -1, 2, -2, 3, -3, 4)
    besides = {j: beside(j, i) for i, j in enumerate(ring)}

    tt = 2 * (y % 2) + c

    def quarter(m):
        q = lax.rem(y // 2 + m, 4)
        k = row(2 * m)
        return q != d, remote(gath.at[k], gd.at[tt, d], z_s.at[m], z_r.at[d], (s, t, q))

    def send_quarter(m):
        away, copy = quarter(m)

        @pl.when(away)
        def _():
            copy.start()

    locals_[2].wait()
    besides[0].start()
    send_quarter(0)

    locals_[1].wait()
    below = (s - 1, t, d)
    early = remote(qkv_in, qkv_u, e_s.at[0], e_r.at[0], below)
    pos_copy = remote(pos_o, pos_u, e_s.at[1], e_r.at[1], below)
    cross = remote(qkv_in.at[pl.ds(0, 3)], qkv_u.at[pl.ds(0, 3)], e_s.at[0], e_r.at[0], below)

    def part(p):
        return pl.ds(1 + 2 * p, 2)

    def to_plane(p):
        return remote(qkv_in.at[part(p)], relay, e_s.at[1 + p], e_r.at[5], (base + p, t, d))

    def from_plane(p):
        return remote(relay, qkv_u.at[part(p)], e_s.at[5], e_r.at[1 + p], (base - 1, t, d))

    @pl.when(x > 0)
    def _():
        early.start()
        pos_copy.start()

    @pl.when(jnp.logical_and(x == 0, crosses))
    def _():
        for p in (1, 2, 3):
            to_plane(p).start()
        cross.start()
        remote(pos_o, pos_u, e_s.at[6], e_r.at[1], below).start()

    locals_[0].wait()
    for h in range(NH):
        p = probs_t(qkv_o, pos_o, h).astype(BF16)
        att[d, :, h * DH:(h + 1) * DH] = dot(p, qkv_o[2 * NH + h], 0, 0).astype(BF16)
    att_copies = [
        remote(att.at[d], att.at[d], a_s.at[i], a_r.at[d], (s, t, lax.rem(d + i, 4))) for i in (1, 2, 3)
    ]
    for copy in att_copies:
        copy.start()

    def add(k, first=False):
        rows = pl.ds(pl.multiple_of(k * COLS, COLS), COLS)
        value = jnp.dot(gath[k], w_v[rows, :], preferred_element_type=F32)
        acc[...] = value if first else acc[...] + value

    locals_[3].wait()
    add(row(0), first=True)

    p2[0].wait_recv()
    p4.start()
    p3[0].start()
    m2[1].wait_recv()
    m4.start()
    m3[1].start()
    p2[1].wait_recv()
    p3[1].start()
    besides[-2].start()
    m2[0].wait_recv()
    m3[0].start()
    besides[2].start()
    send_quarter(1)
    send_quarter(3)
    p1.wait_recv()
    besides[-1].start()
    m1.wait_recv()
    besides[1].start()

    for p in (1, 2, 3):
        @pl.when(jnp.logical_and(x == p, crosses))
        def _(p=p):
            to_plane(p).wait_recv()
            from_plane(p).start()

    for j in (-2, 2, -1, 1):
        add(row(j))

    def other(j):
        besides[j].wait_recv()
        add(row(j, 1 - c))

    for j in (0, -2, 2, -1, 1):
        other(j)

    for q in p3:
        q.wait_recv()
    besides[-3].start()
    add(row(-3))
    for q in m3:
        q.wait_recv()
    besides[3].start()
    add(row(3))
    p4.wait_recv()
    m4.wait_recv()
    besides[4].start()
    send_quarter(2)
    add(row(4))
    for j in (-3, 3, 4):
        other(j)

    d_own[...] = acc[...].astype(BF16)
    late = [remote(d_own.at[r], d_up.at[r], l_s.at[i], l_r.at[i], below) for i, r in enumerate((lo, up))]
    hop = remote(d_own.at[up], relay2, l_s.at[1], l_r.at[2], (base + 3, t, d))
    hop_on = remote(relay2, d_up.at[up], l_s.at[2], l_r.at[1], (base - 1, t, d))

    @pl.when(x > 0)
    def _():
        late[0].start()
        late[1].start()

    @pl.when(jnp.logical_and(x == 0, crosses))
    def _():
        hop.start()
        late[0].start()

    mine = [pltpu.make_async_copy(gath.at[4 * d + i], gd.at[i, d], loc.at[4 + i]) for i in range(4)]
    for copy in mine:
        copy.start()

    has_above = s < 15

    @pl.when(jnp.logical_and(has_above, x < 3))
    def _():
        early.wait_recv()

    @pl.when(jnp.logical_and(has_above, x == 3))
    def _():
        cross.wait_recv()
        for p in (1, 2, 3):
            from_plane(p).wait_recv()

    @pl.when(has_above)
    def _():
        pos_copy.wait_recv()
        for h in range(NH):
            p_up[h] = probs_t(qkv_u, pos_u, h)

    @pl.when(jnp.logical_and(x == 3, crosses))
    def _():
        hop.wait_recv()
        hop_on.start()

    pair = lax.rem(y + 1 - 2 * (y % 2), 8) * 2 + c
    tt2 = 2 * (1 - y % 2) + c
    there, side1, side2 = [], [], []
    for i in (1, 2, 3):
        r = lax.rem(d + i, 4)
        there.append(remote(gd.at[tt, r], gd.at[tt, r], x_s.at[i], x_r.at[r], (s, pair, d)))
        side1.append(remote(gd.at[tt, r], gd.at[tt, r], x_s.at[4 + i], x_r.at[4 + r], (s, sib, d)))
        side2.append(remote(gd.at[tt2, r], gd.at[tt2, r], x_s.at[8 + i], x_r.at[8 + r], (s, sib, d)))
    for i in (1, 2, 3):
        r = lax.rem(d + i, 4)
        remote(gath.at[0], gd.at[tt, r], z_s.at[0], z_r.at[r], (s, t, r)).wait_recv()
        there[i - 1].start()
        side1[i - 1].start()

    @pl.when(has_above)
    def _():
        for copy in late:
            copy.wait_recv()
        scale = 1.0 / math.sqrt(DH)
        for h in range(NH):
            p = p_up[h]
            da = d_up[:, h * DH:(h + 1) * DH]
            dp = dot(qkv_u[2 * NH + h], da, 1, 1)
            ds = (p * (dp - jnp.sum(p * dp, axis=0, keepdims=True))).astype(BF16)
            up_out[2 * NH + h] = dot(p.astype(BF16), da, 1, 0).astype(BF16)
            up_out[NH + h] = (dot(ds, qkv_u[h], 1, 0) * scale).astype(BF16)
            up_out[h] = (dot(ds, qkv_u[NH + h], 0, 0) * scale).astype(BF16)

    @pl.when(jnp.logical_not(has_above))
    def _():
        up_out[...] = jnp.zeros_like(up_out)

    for i in (1, 2, 3):
        r = lax.rem(d + i, 4)
        remote(gd.at[tt2, r], gd.at[tt2, r], x_s.at[i], x_r.at[r], (s, pair, d)).wait_recv()
        side2[i - 1].start()

    for copy in mine:
        copy.wait()
    for i in (1, 2, 3):
        r = lax.rem(d + i, 4)
        remote(att.at[r], att.at[r], a_s.at[i], a_r.at[r], (s, t, r)).wait_recv()
    for copy in side1 + side2:
        copy.wait_recv()
    rows = att[...].reshape(4 * SEQ, COLS)
    for i in range(4):
        dw_out[i * COLS:(i + 1) * COLS, :] = dot(gd[i].reshape(4 * SEQ, COLS), rows, 0, 0).astype(BF16)

    for copy in p2 + m2 + [p1, m1] + p3 + m3 + [p4, m4] + list(besides.values()) + att_copies:
        copy.wait_send()
    for copy in there + side1 + side2:
        copy.wait_send()
    for m in range(4):
        away, copy = quarter(m)

        @pl.when(away)
        def _(copy=copy):
            copy.wait_send()

    @pl.when(x > 0)
    def _():
        early.wait_send()
        pos_copy.wait_send()
        late[0].wait_send()
        late[1].wait_send()

    @pl.when(jnp.logical_and(x == 0, crosses))
    def _():
        for p in (1, 2, 3):
            to_plane(p).wait_send()
        cross.wait_send()
        remote(pos_o, pos_u, e_s.at[6], e_r.at[1], below).wait_send()
        hop.wait_send()
        late[0].wait_send()

    for p in (1, 2, 3):
        @pl.when(jnp.logical_and(x == p, crosses))
        def _(p=p):
            from_plane(p).wait_send()

    @pl.when(jnp.logical_and(x == 3, crosses))
    def _():
        hop_on.wait_send()


def local(saved_qkv, positions, w_out, grad_out):
    qkv = jnp.transpose(saved_qkv[0, 0], (0, 2, 1, 3)).reshape(3 * NH, SEQ, DH)
    sems = pltpu.SemaphoreType.DMA
    any_, vmem = pl.BlockSpec(memory_space=pl.ANY), pl.BlockSpec(memory_space=pltpu.VMEM)
    dw, up = pl.pallas_call(
        kernel,
        out_shape=(
            jax.ShapeDtypeStruct((4 * COLS, COLS), BF16),
            jax.ShapeDtypeStruct((3 * NH, SEQ, DH), BF16),
        ),
        in_specs=[any_] * 4,
        out_specs=(vmem, vmem),
        scratch_shapes=[
            pltpu.VMEM((16, SEQ, COLS), BF16),
            pltpu.VMEM((16 * COLS, COLS), BF16),
            pltpu.VMEM((3 * NH, SEQ, DH), BF16),
            pltpu.VMEM((1, SEQ), jnp.int32),
            pltpu.VMEM((3 * NH, SEQ, DH), BF16),
            pltpu.VMEM((1, SEQ), jnp.int32),
            pltpu.VMEM((2, SEQ, DH), BF16),
            pltpu.VMEM((HALF, COLS), BF16),
            pltpu.VMEM((4, SEQ, COLS), BF16),
            pltpu.VMEM((4, 4, SEQ, COLS), BF16),
            pltpu.VMEM((SEQ, COLS), F32),
            pltpu.VMEM((SEQ, COLS), BF16),
            pltpu.VMEM((SEQ, COLS), BF16),
            pltpu.VMEM((NH, SEQ, SEQ), F32),
            sems((8,)), sems((12,)), sems((12,)), sems((8,)), sems((8,)), sems((4,)), sems((4,)),
            sems((4,)), sems((4,)), sems((7,)), sems((6,)), sems((3,)), sems((3,)), sems((12,)), sems((12,)),
        ],
        compiler_params=pltpu.CompilerParams(
            collective_id=0, has_side_effects=True, vmem_limit_bytes=VMEM_LIMIT
        ),
        cost_estimate=pl.CostEstimate(flops=1_300_000_000, bytes_accessed=7_000_000, transcendentals=100_000),
    )(qkv, positions[0], w_out[0], grad_out[0, 0])
    up = jnp.transpose(up.reshape(3, NH, SEQ, DH), (0, 2, 1, 3))
    return dw[None], up[None, None]


def solution(mesh):
    in_specs = (
        P("section", "dp", None, None, "st", None),
        P("section", "dp", None),
        P("section", None, "st"),
        P("section", "dp", None, "st"),
    )
    out_specs = (P("section", "dp", "st"), P("section", "dp", None, None, "st", None))
    return jax.shard_map(local, mesh=mesh, in_specs=in_specs, out_specs=out_specs, check_vma=False)
```

```python
import math

import jax
import jax.numpy as jnp
from jax import lax
from jax.experimental import pallas as pl
from jax.experimental.pallas import tpu as pltpu
from jax.sharding import PartitionSpec as P

MESH = pl.DeviceIdType.MESH
F32, BF16 = jnp.float32, jnp.bfloat16
SEQ, DH, NH, COLS = 128, 128, 3, 384
HALF = SEQ // 2
VMEM_LIMIT = 32 * 2**20


def dot(a, b, ca, cb):
    return lax.dot_general(a, b, (((ca,), (cb,)), ((), ())), preferred_element_type=F32)


def probs_t(qkv, pos, h):
    scores = dot(qkv[NH + h], qkv[h], 1, 1) * (1.0 / math.sqrt(DH))
    pos_q = jnp.broadcast_to(pos[...], (SEQ, SEQ))
    scores = jnp.where(pos_q.T <= pos_q, scores, -1e30)
    e = jnp.exp(scores - jnp.max(scores, axis=0, keepdims=True))
    return e / jnp.sum(e, axis=0, keepdims=True)


def kernel(
    qkv_in, pos_in, w_in, grad_in, dw_out, up_out,
    gath, w_v, qkv_o, pos_o, qkv_u, pos_u, relay, relay2, att, gd, acc, d_own, d_up, p_up,
    loc, g_s, g_r, b_s, b_r, z_s, z_r, a_s, a_r, e_s, e_r, l_s, l_r, x_s, x_r,
):
    s, t, d = lax.axis_index("section"), lax.axis_index("st"), lax.axis_index("dp")
    y, c = t // 2, t % 2
    x, hi = s % 4, s // 4
    base = hi * 4
    sib = y * 2 + 1 - c
    crosses = hi > 0

    def row(j, core=None):
        return lax.rem(y + 8 + j, 8) * 2 + (c if core is None else core)

    def remote(src, dst, ss, rs, dev):
        return pltpu.make_async_remote_copy(
            src_ref=src, dst_ref=dst, send_sem=ss, recv_sem=rs, device_id=dev, device_id_type=MESH
        )

    bar = pltpu.get_barrier_semaphore()

    def greet(dev):
        pl.semaphore_signal(bar, inc=1, device_id=dev, device_id_type=MESH)

    for j in (1, -1, 2, -2):
        greet((s, row(j), d))
    greet((s, sib, d))
    for i in (1, 2, 3):
        greet((s, t, lax.rem(d + i, 4)))

    @pl.when(x < 3)
    def _():
        greet((s + 1, t, d))

    @pl.when(jnp.logical_and(x > 0, crosses))
    def _():
        greet((base, t, d))

    @pl.when(jnp.logical_and(x == 3, hi < 3))
    def _():
        for i in range(4):
            greet((base + 4 + i, t, d))

    locals_ = [
        pltpu.make_async_copy(qkv_in, qkv_o, loc.at[0]),
        pltpu.make_async_copy(pos_in, pos_o, loc.at[1]),
        pltpu.make_async_copy(grad_in, gath.at[t], loc.at[2]),
        pltpu.make_async_copy(w_in, w_v, loc.at[3]),
    ]
    for copy in locals_:
        copy.start()

    pl.semaphore_wait(bar, 8 + jnp.where(x > 0, 1, 0) + jnp.where(crosses, jnp.where(x > 0, 1, 4), 0))

    lo, up = pl.ds(0, HALF), pl.ds(HALF, HALF)

    def own(j, rows, i):
        return remote(grad_in.at[rows], gath.at[t, rows], g_s.at[i], g_r.at[i], (s, row(j), d))

    def onward(start, j, rows, i):
        k = row(start)
        return remote(gath.at[k, rows], gath.at[k, rows], g_s.at[i], g_r.at[i], (s, row(j), d))

    p2 = [own(2, lo, 0), own(2, up, 1)]
    m2 = [own(-2, lo, 2), own(-2, up, 3)]
    p1, m1 = own(1, pl.ds(0, SEQ), 4), own(-1, pl.ds(0, SEQ), 5)
    p3 = [onward(-2, 1, lo, 6), onward(-2, 1, up, 7)]
    m3 = [onward(2, -1, lo, 8), onward(2, -1, up, 9)]
    p4, m4 = onward(-2, 2, lo, 10), onward(2, -2, up, 11)

    p2[0].start()
    m2[1].start()
    p2[1].start()
    m2[0].start()
    p1.start()
    m1.start()

    def beside(j, i):
        k = row(j)
        return remote(gath.at[k], gath.at[k], b_s.at[i], b_r.at[i], (s, sib, d))

    ring = (0, 1, -1, 2, -2, 3, -3, 4)
    besides = {j: beside(j, i) for i, j in enumerate(ring)}

    tt = 2 * (y % 2) + c

    def quarter(m):
        q = lax.rem(y // 2 + m, 4)
        k = row(2 * m)
        return q != d, remote(gath.at[k], gd.at[tt, d], z_s.at[m], z_r.at[d], (s, t, q))

    def send_quarter(m):
        away, copy = quarter(m)

        @pl.when(away)
        def _():
            copy.start()

    locals_[2].wait()
    besides[0].start()
    send_quarter(0)

    locals_[1].wait()
    below = (s - 1, t, d)
    early = remote(qkv_in, qkv_u, e_s.at[0], e_r.at[0], below)
    pos_copy = remote(pos_o, pos_u, e_s.at[1], e_r.at[1], below)
    cross = remote(qkv_in.at[pl.ds(0, 3)], qkv_u.at[pl.ds(0, 3)], e_s.at[0], e_r.at[0], below)

    def part(p):
        return pl.ds(1 + 2 * p, 2)

    def to_plane(p):
        return remote(qkv_in.at[part(p)], relay, e_s.at[1 + p], e_r.at[5], (base + p, t, d))

    def from_plane(p):
        return remote(relay, qkv_u.at[part(p)], e_s.at[5], e_r.at[1 + p], (base - 1, t, d))

    @pl.when(x > 0)
    def _():
        early.start()
        pos_copy.start()

    @pl.when(jnp.logical_and(x == 0, crosses))
    def _():
        for p in (1, 2, 3):
            to_plane(p).start()
        cross.start()
        remote(pos_o, pos_u, e_s.at[6], e_r.at[1], below).start()

    locals_[0].wait()
    for h in range(NH):
        p = probs_t(qkv_o, pos_o, h).astype(BF16)
        att[d, :, h * DH:(h + 1) * DH] = dot(p, qkv_o[2 * NH + h], 0, 0).astype(BF16)

    def pass_att(k, step, i):
        r = d - k * step
        return remote(att.at[r], att.at[r], a_s.at[i], a_r.at[r], (s, t, d + step))

    lines = ((1, d < 3), (-1, d > 0))

    def source(k, step):
        return (d >= k) if step == 1 else (d + k < 4)

    for i, (step, more) in enumerate(lines):
        @pl.when(more)
        def _(i=i, step=step):
            pass_att(0, step, i).start()

    def relay_att(k):
        for i, (step, more) in enumerate(lines):
            @pl.when(source(k, step))
            def _(step=step):
                pass_att(k, step, 0).wait_recv()

            if k < 3:
                @pl.when(jnp.logical_and(source(k, step), more))
                def _(i=i, step=step):
                    pass_att(k, step, 2 * k + i).start()

    def add(k, first=False):
        rows = pl.ds(pl.multiple_of(k * COLS, COLS), COLS)
        value = jnp.dot(gath[k], w_v[rows, :], preferred_element_type=F32)
        acc[...] = value if first else acc[...] + value

    locals_[3].wait()
    add(row(0), first=True)

    p2[0].wait_recv()
    p4.start()
    p3[0].start()
    m2[1].wait_recv()
    m4.start()
    m3[1].start()
    p2[1].wait_recv()
    p3[1].start()
    besides[-2].start()
    m2[0].wait_recv()
    m3[0].start()
    besides[2].start()
    send_quarter(1)
    send_quarter(3)
    p1.wait_recv()
    besides[-1].start()
    m1.wait_recv()
    besides[1].start()

    for p in (1, 2, 3):
        @pl.when(jnp.logical_and(x == p, crosses))
        def _(p=p):
            to_plane(p).wait_recv()
            from_plane(p).start()

    for j in (-2, 2, -1, 1):
        add(row(j))

    def other(j):
        besides[j].wait_recv()
        add(row(j, 1 - c))

    for j in (0, -2, 2, -1, 1):
        other(j)
    relay_att(1)

    for q in p3:
        q.wait_recv()
    besides[-3].start()
    add(row(-3))
    for q in m3:
        q.wait_recv()
    besides[3].start()
    add(row(3))
    p4.wait_recv()
    m4.wait_recv()
    besides[4].start()
    send_quarter(2)
    add(row(4))
    for j in (-3, 3, 4):
        other(j)

    d_own[...] = acc[...].astype(BF16)
    late = [remote(d_own.at[r], d_up.at[r], l_s.at[i], l_r.at[i], below) for i, r in enumerate((lo, up))]
    hop = remote(d_own.at[up], relay2, l_s.at[1], l_r.at[2], (base + 1, t, d))
    hop_on = remote(relay2, d_up.at[up], l_s.at[2], l_r.at[1], (base - 1, t, d))

    @pl.when(x > 0)
    def _():
        late[0].start()
        late[1].start()

    @pl.when(jnp.logical_and(x == 0, crosses))
    def _():
        hop.start()
        late[0].start()

    mine = [pltpu.make_async_copy(gath.at[4 * d + i], gd.at[i, d], loc.at[4 + i]) for i in range(4)]
    for copy in mine:
        copy.start()

    has_above = s < 15

    def softmax_above():
        pos_copy.wait_recv()
        for h in range(NH):
            p_up[h] = probs_t(qkv_u, pos_u, h)

    def backward_above():
        for copy in late:
            copy.wait_recv()
        scale = 1.0 / math.sqrt(DH)
        for h in range(NH):
            p = p_up[h]
            da = d_up[:, h * DH:(h + 1) * DH]
            dp = dot(qkv_u[2 * NH + h], da, 1, 1)
            ds = (p * (dp - jnp.sum(p * dp, axis=0, keepdims=True))).astype(BF16)
            up_out[2 * NH + h] = dot(p.astype(BF16), da, 1, 0).astype(BF16)
            up_out[NH + h] = (dot(ds, qkv_u[h], 1, 0) * scale).astype(BF16)
            up_out[h] = (dot(ds, qkv_u[NH + h], 0, 0) * scale).astype(BF16)

    @pl.when(x < 3)
    def _():
        early.wait_recv()
        softmax_above()

    @pl.when(jnp.logical_and(x == 1, crosses))
    def _():
        hop.wait_recv()
        hop_on.start()

    relay_att(2)

    pair = (y + 1 - 2 * (y % 2)) * 2 + c
    tt2 = 2 * (1 - y % 2) + c
    others = (d + 1 - 2 * (d % 2), 2 - d // 2, 3 - 3 * (d // 2))
    there, side1, side2 = [], [], []
    for i, r in enumerate(others):
        there.append(remote(gd.at[tt, r], gd.at[tt, r], x_s.at[i], x_r.at[r], (s, pair, d)))
        side1.append(remote(gd.at[tt, r], gd.at[tt, r], x_s.at[4 + i], x_r.at[4 + r], (s, sib, d)))
        side2.append(remote(gd.at[tt2, r], gd.at[tt2, r], x_s.at[8 + i], x_r.at[8 + r], (s, sib, d)))
    for i, r in enumerate(others):
        remote(gath.at[0], gd.at[tt, r], z_s.at[0], z_r.at[r], (s, t, r)).wait_recv()
        there[i].start()
        side1[i].start()

    @pl.when(x < 3)
    def _():
        backward_above()

    for i, r in enumerate(others):
        remote(gd.at[tt2, r], gd.at[tt2, r], x_s.at[i], x_r.at[r], (s, pair, d)).wait_recv()
        side2[i].start()

    for copy in mine:
        copy.wait()
    relay_att(3)
    for copy in side1 + side2:
        copy.wait_recv()
    rows = att[...].reshape(4 * SEQ, COLS)
    for i in range(4):
        dw_out[i * COLS:(i + 1) * COLS, :] = dot(gd[i].reshape(4 * SEQ, COLS), rows, 0, 0).astype(BF16)

    @pl.when(jnp.logical_and(x == 3, has_above))
    def _():
        cross.wait_recv()
        for p in (1, 2, 3):
            from_plane(p).wait_recv()
        softmax_above()
        backward_above()

    @pl.when(jnp.logical_not(has_above))
    def _():
        up_out[...] = jnp.zeros_like(up_out)

    for copy in p2 + m2 + [p1, m1] + p3 + m3 + [p4, m4] + list(besides.values()):
        copy.wait_send()
    for copy in there + side1 + side2:
        copy.wait_send()
    for m in range(4):
        away, copy = quarter(m)

        @pl.when(away)
        def _(copy=copy):
            copy.wait_send()

    for k in range(3):
        for i, (step, more) in enumerate(lines):
            @pl.when(jnp.logical_and(source(k, step), more))
            def _(k=k, i=i, step=step):
                pass_att(k, step, 2 * k + i).wait_send()

    @pl.when(x > 0)
    def _():
        early.wait_send()
        pos_copy.wait_send()
        late[0].wait_send()
        late[1].wait_send()

    @pl.when(jnp.logical_and(x == 0, crosses))
    def _():
        for p in (1, 2, 3):
            to_plane(p).wait_send()
        cross.wait_send()
        remote(pos_o, pos_u, e_s.at[6], e_r.at[1], below).wait_send()
        hop.wait_send()
        late[0].wait_send()

    for p in (1, 2, 3):
        @pl.when(jnp.logical_and(x == p, crosses))
        def _(p=p):
            from_plane(p).wait_send()

    @pl.when(jnp.logical_and(x == 1, crosses))
    def _():
        hop_on.wait_send()


def local(saved_qkv, positions, w_out, grad_out):
    qkv = jnp.transpose(saved_qkv[0, 0], (0, 2, 1, 3)).reshape(3 * NH, SEQ, DH)
    sems = pltpu.SemaphoreType.DMA
    any_, vmem = pl.BlockSpec(memory_space=pl.ANY), pl.BlockSpec(memory_space=pltpu.VMEM)
    dw, up = pl.pallas_call(
        kernel,
        out_shape=(
            jax.ShapeDtypeStruct((4 * COLS, COLS), BF16),
            jax.ShapeDtypeStruct((3 * NH, SEQ, DH), BF16),
        ),
        in_specs=[any_] * 4,
        out_specs=(vmem, vmem),
        scratch_shapes=[
            pltpu.VMEM((16, SEQ, COLS), BF16),
            pltpu.VMEM((16 * COLS, COLS), BF16),
            pltpu.VMEM((3 * NH, SEQ, DH), BF16),
            pltpu.VMEM((1, SEQ), jnp.int32),
            pltpu.VMEM((3 * NH, SEQ, DH), BF16),
            pltpu.VMEM((1, SEQ), jnp.int32),
            pltpu.VMEM((2, SEQ, DH), BF16),
            pltpu.VMEM((HALF, COLS), BF16),
            pltpu.VMEM((4, SEQ, COLS), BF16),
            pltpu.VMEM((4, 4, SEQ, COLS), BF16),
            pltpu.VMEM((SEQ, COLS), F32),
            pltpu.VMEM((SEQ, COLS), BF16),
            pltpu.VMEM((SEQ, COLS), BF16),
            pltpu.VMEM((NH, SEQ, SEQ), F32),
            sems((8,)), sems((12,)), sems((12,)), sems((8,)), sems((8,)), sems((4,)), sems((4,)),
            sems((6,)), sems((4,)), sems((7,)), sems((6,)), sems((3,)), sems((3,)), sems((12,)), sems((12,)),
        ],
        compiler_params=pltpu.CompilerParams(
            collective_id=0, has_side_effects=True, vmem_limit_bytes=VMEM_LIMIT
        ),
        cost_estimate=pl.CostEstimate(flops=1_300_000_000, bytes_accessed=7_000_000, transcendentals=100_000),
    )(*(pltpu.with_memory_space_constraint(a, pltpu.HBM) for a in (qkv, positions[0], w_out[0], grad_out[0, 0])))
    up = jnp.transpose(up.reshape(3, NH, SEQ, DH), (0, 2, 1, 3))
    return dw[None], up[None, None]


def solution(mesh):
    in_specs = (
        P("section", "dp", None, None, "st", None),
        P("section", "dp", None),
        P("section", None, "st"),
        P("section", "dp", None, "st"),
    )
    out_specs = (P("section", "dp", "st"), P("section", "dp", None, None, "st", None))
    return jax.shard_map(local, mesh=mesh, in_specs=in_specs, out_specs=out_specs, check_vma=False)
```

```python
import math

import jax
import jax.numpy as jnp
from jax import lax
from jax.experimental import pallas as pl
from jax.experimental.pallas import tpu as pltpu
from jax.sharding import PartitionSpec as P

MESH = pl.DeviceIdType.MESH
F32, BF16 = jnp.float32, jnp.bfloat16
SEQ, DH, NH, COLS = 128, 128, 3, 384
HALF = SEQ // 2
NEAR = 80
VMEM_LIMIT = 32 * 2**20


def dot(a, b, ca, cb):
    return lax.dot_general(a, b, (((ca,), (cb,)), ((), ())), preferred_element_type=F32)


def probs_t(qkv, pos, h):
    scores = dot(qkv[NH + h], qkv[h], 1, 1) * (1.0 / math.sqrt(DH))
    pos_q = jnp.broadcast_to(pos[...], (SEQ, SEQ))
    scores = jnp.where(pos_q.T <= pos_q, scores, -1e30)
    e = jnp.exp(scores - jnp.max(scores, axis=0, keepdims=True))
    return e / jnp.sum(e, axis=0, keepdims=True)


def kernel(
    qkv_in, pos_in, w_in, grad_in, dw_out, up_out,
    gath, w_v, qkv_o, pos_o, qkv_u, pos_u, relay, relay2, att, gd, acc, d_own, d_up, p_up,
    loc, g_s, g_r, b_s, b_r, z_s, z_r, a_s, a_r, e_s, e_r, l_s, l_r, x_s, x_r,
):
    s, t, d = lax.axis_index("section"), lax.axis_index("st"), lax.axis_index("dp")
    y, c = t // 2, t % 2
    x, hi = s % 4, s // 4
    base = hi * 4
    sib = y * 2 + 1 - c
    crosses = hi > 0

    def row(j, core=None):
        return lax.rem(y + 8 + j, 8) * 2 + (c if core is None else core)

    def remote(src, dst, ss, rs, dev):
        return pltpu.make_async_remote_copy(
            src_ref=src, dst_ref=dst, send_sem=ss, recv_sem=rs, device_id=dev, device_id_type=MESH
        )

    bar = pltpu.get_barrier_semaphore()

    def greet(dev):
        pl.semaphore_signal(bar, inc=1, device_id=dev, device_id_type=MESH)

    for j in (1, -1, 2, -2):
        greet((s, row(j), d))
    greet((s, sib, d))
    for i in (1, 2, 3):
        greet((s, t, lax.rem(d + i, 4)))

    @pl.when(x < 3)
    def _():
        greet((s + 1, t, d))

    @pl.when(jnp.logical_and(x > 0, crosses))
    def _():
        greet((base, t, d))

    @pl.when(jnp.logical_and(x == 3, hi < 3))
    def _():
        for i in range(4):
            greet((base + 4 + i, t, d))

    locals_ = [
        pltpu.make_async_copy(qkv_in, qkv_o, loc.at[0]),
        pltpu.make_async_copy(pos_in, pos_o, loc.at[1]),
        pltpu.make_async_copy(grad_in, gath.at[t], loc.at[2]),
        pltpu.make_async_copy(w_in, w_v, loc.at[3]),
    ]
    for copy in locals_:
        copy.start()

    pl.semaphore_wait(bar, 8 + jnp.where(x > 0, 1, 0) + jnp.where(crosses, jnp.where(x > 0, 1, 4), 0))

    lo, up = pl.ds(0, HALF), pl.ds(HALF, HALF)

    def own(j, rows, i):
        return remote(grad_in.at[rows], gath.at[t, rows], g_s.at[i], g_r.at[i], (s, row(j), d))

    def onward(start, j, rows, i):
        k = row(start)
        return remote(gath.at[k, rows], gath.at[k, rows], g_s.at[i], g_r.at[i], (s, row(j), d))

    p2 = [own(2, lo, 0), own(2, up, 1)]
    m2 = [own(-2, lo, 2), own(-2, up, 3)]
    p1, m1 = own(1, pl.ds(0, SEQ), 4), own(-1, pl.ds(0, SEQ), 5)
    p3 = [onward(-2, 1, lo, 6), onward(-2, 1, up, 7)]
    m3 = [onward(2, -1, lo, 8), onward(2, -1, up, 9)]
    p4, m4 = onward(-2, 2, lo, 10), onward(2, -2, up, 11)

    p2[0].start()
    m2[1].start()
    p2[1].start()
    m2[0].start()
    p1.start()
    m1.start()

    def beside(j, i):
        k = row(j)
        return remote(gath.at[k], gath.at[k], b_s.at[i], b_r.at[i], (s, sib, d))

    ring = (0, 1, -1, 2, -2, 3, -3, 4)
    besides = {j: beside(j, i) for i, j in enumerate(ring)}

    tt = 2 * (y % 2) + c

    def quarter(m):
        q = lax.rem(y // 2 + m, 4)
        k = row(2 * m)
        return q != d, remote(gath.at[k], gd.at[tt, d], z_s.at[m], z_r.at[d], (s, t, q))

    def send_quarter(m):
        away, copy = quarter(m)

        @pl.when(away)
        def _():
            copy.start()

    locals_[2].wait()
    besides[0].start()
    send_quarter(0)

    locals_[1].wait()
    below = (s - 1, t, d)
    early = remote(qkv_in, qkv_u, e_s.at[0], e_r.at[0], below)
    pos_copy = remote(pos_o, pos_u, e_s.at[1], e_r.at[1], below)
    cross = remote(qkv_in.at[pl.ds(0, 3)], qkv_u.at[pl.ds(0, 3)], e_s.at[0], e_r.at[0], below)

    def part(p):
        return pl.ds(1 + 2 * p, 2)

    def to_plane(p):
        return remote(qkv_in.at[part(p)], relay, e_s.at[1 + p], e_r.at[5], (base + p, t, d))

    def from_plane(p):
        return remote(relay, qkv_u.at[part(p)], e_s.at[5], e_r.at[1 + p], (base - 1, t, d))

    @pl.when(x > 0)
    def _():
        early.start()
        pos_copy.start()

    @pl.when(jnp.logical_and(x == 0, crosses))
    def _():
        for p in (1, 2, 3):
            to_plane(p).start()
        cross.start()
        remote(pos_o, pos_u, e_s.at[6], e_r.at[1], below).start()

    locals_[0].wait()
    for h in range(NH):
        p = probs_t(qkv_o, pos_o, h).astype(BF16)
        att[d, :, h * DH:(h + 1) * DH] = dot(p, qkv_o[2 * NH + h], 0, 0).astype(BF16)

    def pass_att(k, step, i):
        r = d - k * step
        return remote(att.at[r], att.at[r], a_s.at[i], a_r.at[r], (s, t, d + step))

    lines = ((1, d < 3), (-1, d > 0))

    def source(k, step):
        return (d >= k) if step == 1 else (d + k < 4)

    for i, (step, more) in enumerate(lines):
        @pl.when(more)
        def _(i=i, step=step):
            pass_att(0, step, i).start()

    def relay_att(k):
        for i, (step, more) in enumerate(lines):
            @pl.when(source(k, step))
            def _(step=step):
                pass_att(k, step, 0).wait_recv()

            if k < 3:
                @pl.when(jnp.logical_and(source(k, step), more))
                def _(i=i, step=step):
                    pass_att(k, step, 2 * k + i).start()

    def add(k, first=False):
        rows = pl.ds(pl.multiple_of(k * COLS, COLS), COLS)
        value = jnp.dot(gath[k], w_v[rows, :], preferred_element_type=F32)
        acc[...] = value if first else acc[...] + value

    locals_[3].wait()
    add(row(0), first=True)

    p2[0].wait_recv()
    p4.start()
    p3[0].start()
    m2[1].wait_recv()
    m4.start()
    m3[1].start()
    p2[1].wait_recv()
    p3[1].start()
    besides[-2].start()
    m2[0].wait_recv()
    m3[0].start()
    besides[2].start()
    send_quarter(1)
    send_quarter(3)
    p1.wait_recv()
    besides[-1].start()
    m1.wait_recv()
    besides[1].start()

    for p in (1, 2, 3):
        @pl.when(jnp.logical_and(x == p, crosses))
        def _(p=p):
            to_plane(p).wait_recv()
            from_plane(p).start()

    for j in (-2, 2, -1, 1):
        add(row(j))

    def other(j):
        besides[j].wait_recv()
        add(row(j, 1 - c))

    for j in (0, -2, 2, -1, 1):
        other(j)
    relay_att(1)

    for q in p3:
        q.wait_recv()
    besides[-3].start()
    add(row(-3))
    for q in m3:
        q.wait_recv()
    besides[3].start()
    add(row(3))
    p4.wait_recv()
    m4.wait_recv()
    besides[4].start()
    send_quarter(2)
    add(row(4))
    for j in (-3, 3, 4):
        other(j)

    d_own[...] = acc[...].astype(BF16)
    near, far = pl.ds(0, NEAR), pl.ds(NEAR, SEQ - NEAR)
    late = [remote(d_own.at[r], d_up.at[r], l_s.at[i], l_r.at[i], below) for i, r in enumerate((near, far))]
    hop = remote(d_own.at[far], relay2, l_s.at[1], l_r.at[2], (base + 3, t, d))
    hop_on = remote(relay2, d_up.at[far], l_s.at[2], l_r.at[1], (base - 1, t, d))

    @pl.when(x > 0)
    def _():
        late[0].start()
        late[1].start()

    @pl.when(jnp.logical_and(x == 0, crosses))
    def _():
        hop.start()
        late[0].start()

    mine = [pltpu.make_async_copy(gath.at[4 * d + i], gd.at[i, d], loc.at[4 + i]) for i in range(4)]
    for copy in mine:
        copy.start()

    has_above = s < 15

    def softmax_above():
        pos_copy.wait_recv()
        for h in range(NH):
            p_up[h] = probs_t(qkv_u, pos_u, h)

    def backward_above():
        for copy in late:
            copy.wait_recv()
        scale = 1.0 / math.sqrt(DH)
        for h in range(NH):
            p = p_up[h]
            da = d_up[:, h * DH:(h + 1) * DH]
            dp = dot(qkv_u[2 * NH + h], da, 1, 1)
            ds = (p * (dp - jnp.sum(p * dp, axis=0, keepdims=True))).astype(BF16)
            up_out[2 * NH + h] = dot(p.astype(BF16), da, 1, 0).astype(BF16)
            up_out[NH + h] = (dot(ds, qkv_u[h], 1, 0) * scale).astype(BF16)
            up_out[h] = (dot(ds, qkv_u[NH + h], 0, 0) * scale).astype(BF16)

    @pl.when(x < 3)
    def _():
        early.wait_recv()
        softmax_above()

    @pl.when(jnp.logical_and(x == 3, crosses))
    def _():
        hop.wait_recv()
        hop_on.start()

    relay_att(2)

    turn = 1 - 2 * (y % 2)
    pair, outer = row(turn), row(-turn)
    tt2 = 2 * (1 - y % 2) + c
    others = (d + 1 - 2 * (d % 2), 2 - d // 2, 3 - 3 * (d // 2))
    whole = pl.ds(0, SEQ)

    def swap(tile):
        cuts = ((0, whole, pair), (1, whole, outer), (2, lo, pair), (2, up, outer))
        return [
            remote(gd.at[tile, others[i], rows], gd.at[tile, others[i], rows], x_s.at[n], x_r.at[n], (s, dev, d))
            for n, (i, rows, dev) in enumerate(cuts)
        ]

    def across(tile, n):
        return [
            remote(gd.at[tile, r], gd.at[tile, r], x_s.at[n + i], x_r.at[n + i], (s, sib, d))
            for i, r in enumerate(others)
        ]

    there, missing, side1, side2 = swap(tt), swap(tt2), across(tt, 4), across(tt2, 8)
    sent_on = ((0,), (1,), (2, 3))
    for i, r in enumerate(others):
        remote(gath.at[0], gd.at[tt, r], z_s.at[0], z_r.at[r], (s, t, r)).wait_recv()
        for n in sent_on[i]:
            there[n].start()
        side1[i].start()

    @pl.when(x < 3)
    def _():
        backward_above()

    for i, r in enumerate(others):
        for n in sent_on[i]:
            missing[n].wait_recv()
        side2[i].start()

    for copy in mine:
        copy.wait()
    relay_att(3)
    for copy in side1 + side2:
        copy.wait_recv()
    rows = att[...].reshape(4 * SEQ, COLS)
    for i in range(4):
        dw_out[i * COLS:(i + 1) * COLS, :] = dot(gd[i].reshape(4 * SEQ, COLS), rows, 0, 0).astype(BF16)

    @pl.when(jnp.logical_and(x == 3, has_above))
    def _():
        cross.wait_recv()
        for p in (1, 2, 3):
            from_plane(p).wait_recv()
        softmax_above()
        backward_above()

    @pl.when(jnp.logical_not(has_above))
    def _():
        up_out[...] = jnp.zeros_like(up_out)

    for copy in p2 + m2 + [p1, m1] + p3 + m3 + [p4, m4] + list(besides.values()):
        copy.wait_send()
    for copy in there + side1 + side2:
        copy.wait_send()
    for m in range(4):
        away, copy = quarter(m)

        @pl.when(away)
        def _(copy=copy):
            copy.wait_send()

    for k in range(3):
        for i, (step, more) in enumerate(lines):
            @pl.when(jnp.logical_and(source(k, step), more))
            def _(k=k, i=i, step=step):
                pass_att(k, step, 2 * k + i).wait_send()

    @pl.when(x > 0)
    def _():
        early.wait_send()
        pos_copy.wait_send()
        late[0].wait_send()
        late[1].wait_send()

    @pl.when(jnp.logical_and(x == 0, crosses))
    def _():
        for p in (1, 2, 3):
            to_plane(p).wait_send()
        cross.wait_send()
        remote(pos_o, pos_u, e_s.at[6], e_r.at[1], below).wait_send()
        hop.wait_send()
        late[0].wait_send()

    for p in (1, 2, 3):
        @pl.when(jnp.logical_and(x == p, crosses))
        def _(p=p):
            from_plane(p).wait_send()

    @pl.when(jnp.logical_and(x == 3, crosses))
    def _():
        hop_on.wait_send()


def local(saved_qkv, positions, w_out, grad_out):
    qkv = jnp.transpose(saved_qkv[0, 0], (0, 2, 1, 3)).reshape(3 * NH, SEQ, DH)
    sems = pltpu.SemaphoreType.DMA
    any_, vmem = pl.BlockSpec(memory_space=pl.ANY), pl.BlockSpec(memory_space=pltpu.VMEM)
    dw, up = pl.pallas_call(
        kernel,
        out_shape=(
            jax.ShapeDtypeStruct((4 * COLS, COLS), BF16),
            jax.ShapeDtypeStruct((3 * NH, SEQ, DH), BF16),
        ),
        in_specs=[any_] * 4,
        out_specs=(vmem, vmem),
        scratch_shapes=[
            pltpu.VMEM((16, SEQ, COLS), BF16),
            pltpu.VMEM((16 * COLS, COLS), BF16),
            pltpu.VMEM((3 * NH, SEQ, DH), BF16),
            pltpu.VMEM((1, SEQ), jnp.int32),
            pltpu.VMEM((3 * NH, SEQ, DH), BF16),
            pltpu.VMEM((1, SEQ), jnp.int32),
            pltpu.VMEM((2, SEQ, DH), BF16),
            pltpu.VMEM((SEQ - NEAR, COLS), BF16),
            pltpu.VMEM((4, SEQ, COLS), BF16),
            pltpu.VMEM((4, 4, SEQ, COLS), BF16),
            pltpu.VMEM((SEQ, COLS), F32),
            pltpu.VMEM((SEQ, COLS), BF16),
            pltpu.VMEM((SEQ, COLS), BF16),
            pltpu.VMEM((NH, SEQ, SEQ), F32),
            sems((8,)), sems((12,)), sems((12,)), sems((8,)), sems((8,)), sems((4,)), sems((4,)),
            sems((6,)), sems((4,)), sems((7,)), sems((6,)), sems((3,)), sems((3,)), sems((12,)), sems((12,)),
        ],
        compiler_params=pltpu.CompilerParams(
            collective_id=0, has_side_effects=True, vmem_limit_bytes=VMEM_LIMIT
        ),
        cost_estimate=pl.CostEstimate(flops=1_300_000_000, bytes_accessed=7_000_000, transcendentals=100_000),
    )(*(pltpu.with_memory_space_constraint(a, pltpu.HBM) for a in (qkv, positions[0], w_out[0], grad_out[0, 0])))
    up = jnp.transpose(up.reshape(3, NH, SEQ, DH), (0, 2, 1, 3))
    return dw[None], up[None, None]


def solution(mesh):
    in_specs = (
        P("section", "dp", None, None, "st", None),
        P("section", "dp", None),
        P("section", None, "st"),
        P("section", "dp", None, "st"),
    )
    out_specs = (P("section", "dp", "st"), P("section", "dp", None, None, "st", None))
    return jax.shard_map(local, mesh=mesh, in_specs=in_specs, out_specs=out_specs, check_vma=False)
```

```python
import math

import jax
import jax.numpy as jnp
from jax import lax
from jax.experimental import pallas as pl
from jax.experimental.pallas import tpu as pltpu
from jax.sharding import PartitionSpec as P

MESH = pl.DeviceIdType.MESH
F32, BF16 = jnp.float32, jnp.bfloat16
SEQ, DH, NH, COLS = 128, 128, 3, 384
HALF = SEQ // 2
NEAR = 80
PLANES = {1: (1, 3), 2: (4, 3), 3: (7, 2)}
VMEM_LIMIT = 32 * 2**20


def dot(a, b, ca, cb):
    return lax.dot_general(a, b, (((ca,), (cb,)), ((), ())), preferred_element_type=F32)


def probs_t(qkv, pos, h):
    scores = dot(qkv[NH + h], qkv[h], 1, 1) * (1.0 / math.sqrt(DH))
    pos_q = jnp.broadcast_to(pos[...], (SEQ, SEQ))
    scores = jnp.where(pos_q.T <= pos_q, scores, -1e30)
    e = jnp.exp(scores - jnp.max(scores, axis=0, keepdims=True))
    return e / jnp.sum(e, axis=0, keepdims=True)


def kernel(
    qkv_in, pos_in, w_in, grad_in, dw_out, up_out,
    gath, w_v, qkv_o, pos_o, qkv_u, pos_u, relay, relay2, att, gd, acc, d_own, d_up, p_up,
    loc, g_s, g_r, b_s, b_r, z_s, z_r, a_s, a_r, e_s, e_r, l_s, l_r, x_s, x_r,
):
    s, t, d = lax.axis_index("section"), lax.axis_index("st"), lax.axis_index("dp")
    y, c = t // 2, t % 2
    x, hi = s % 4, s // 4
    base = hi * 4
    sib = y * 2 + 1 - c
    crosses = hi > 0

    def row(j, core=None):
        return lax.rem(y + 8 + j, 8) * 2 + (c if core is None else core)

    def remote(src, dst, ss, rs, dev):
        return pltpu.make_async_remote_copy(
            src_ref=src, dst_ref=dst, send_sem=ss, recv_sem=rs, device_id=dev, device_id_type=MESH
        )

    bar = pltpu.get_barrier_semaphore()

    def greet(dev):
        pl.semaphore_signal(bar, inc=1, device_id=dev, device_id_type=MESH)

    for j in (1, -1, 2, -2):
        greet((s, row(j), d))
    greet((s, sib, d))
    for i in (1, 2, 3):
        greet((s, t, lax.rem(d + i, 4)))

    @pl.when(x < 3)
    def _():
        greet((s + 1, t, d))

    @pl.when(jnp.logical_and(x > 0, crosses))
    def _():
        greet((base, t, d))

    @pl.when(jnp.logical_and(x == 3, hi < 3))
    def _():
        for i in range(4):
            greet((base + 4 + i, t, d))

    locals_ = [
        pltpu.make_async_copy(qkv_in, qkv_o, loc.at[0]),
        pltpu.make_async_copy(pos_in, pos_o, loc.at[1]),
        pltpu.make_async_copy(grad_in, gath.at[t], loc.at[2]),
        pltpu.make_async_copy(w_in, w_v, loc.at[3]),
    ]
    for copy in locals_:
        copy.start()

    pl.semaphore_wait(bar, 8 + jnp.where(x > 0, 1, 0) + jnp.where(crosses, jnp.where(x > 0, 1, 4), 0))

    lo, up = pl.ds(0, HALF), pl.ds(HALF, HALF)

    def own(j, rows, i):
        return remote(grad_in.at[rows], gath.at[t, rows], g_s.at[i], g_r.at[i], (s, row(j), d))

    def onward(start, j, rows, i):
        k = row(start)
        return remote(gath.at[k, rows], gath.at[k, rows], g_s.at[i], g_r.at[i], (s, row(j), d))

    p2 = [own(2, lo, 0), own(2, up, 1)]
    m2 = [own(-2, lo, 2), own(-2, up, 3)]
    p1, m1 = own(1, pl.ds(0, SEQ), 4), own(-1, pl.ds(0, SEQ), 5)
    p3 = [onward(-2, 1, lo, 6), onward(-2, 1, up, 7)]
    m3 = [onward(2, -1, lo, 8), onward(2, -1, up, 9)]
    p4, m4 = onward(-2, 2, lo, 10), onward(2, -2, up, 11)

    p2[0].start()
    m2[1].start()
    p2[1].start()
    m2[0].start()
    p1.start()
    m1.start()

    def beside(j, i):
        k = row(j)
        return remote(gath.at[k], gath.at[k], b_s.at[i], b_r.at[i], (s, sib, d))

    ring = (0, 1, -1, 2, -2, 3, -3, 4)
    besides = {j: beside(j, i) for i, j in enumerate(ring)}

    tt = 2 * (y % 2) + c

    def quarter(m):
        q = lax.rem(y // 2 + m, 4)
        k = row(2 * m)
        return q != d, remote(gath.at[k], gd.at[tt, d], z_s.at[m], z_r.at[d], (s, t, q))

    def send_quarter(m):
        away, copy = quarter(m)

        @pl.when(away)
        def _():
            copy.start()

    locals_[2].wait()
    besides[0].start()
    send_quarter(0)

    locals_[1].wait()
    below = (s - 1, t, d)
    early = remote(qkv_in, qkv_u, e_s.at[0], e_r.at[0], below)
    pos_copy = remote(pos_o, pos_u, e_s.at[1], e_r.at[1], below)
    cross = remote(qkv_in.at[pl.ds(0, 1)], qkv_u.at[pl.ds(0, 1)], e_s.at[0], e_r.at[0], below)

    def part(p):
        return pl.ds(*PLANES[p])

    def to_plane(p):
        return remote(qkv_in.at[part(p)], relay.at[pl.ds(0, PLANES[p][1])], e_s.at[1 + p], e_r.at[5], (base + p, t, d))

    def from_plane(p):
        return remote(relay.at[pl.ds(0, PLANES[p][1])], qkv_u.at[part(p)], e_s.at[5], e_r.at[1 + p], (base - 1, t, d))

    @pl.when(x > 0)
    def _():
        early.start()
        pos_copy.start()

    @pl.when(jnp.logical_and(x == 0, crosses))
    def _():
        for p in (1, 2, 3):
            to_plane(p).start()
        cross.start()
        remote(pos_o, pos_u, e_s.at[6], e_r.at[1], below).start()

    locals_[0].wait()
    for h in range(NH):
        p = probs_t(qkv_o, pos_o, h).astype(BF16)
        att[d, :, h * DH:(h + 1) * DH] = dot(p, qkv_o[2 * NH + h], 0, 0).astype(BF16)

    def pass_att(k, step, i):
        r = d - k * step
        return remote(att.at[r], att.at[r], a_s.at[i], a_r.at[r], (s, t, d + step))

    lines = ((1, d < 3), (-1, d > 0))

    def source(k, step):
        return (d >= k) if step == 1 else (d + k < 4)

    for i, (step, more) in enumerate(lines):
        @pl.when(more)
        def _(i=i, step=step):
            pass_att(0, step, i).start()

    def relay_att(k):
        for i, (step, more) in enumerate(lines):
            @pl.when(source(k, step))
            def _(step=step):
                pass_att(k, step, 0).wait_recv()

            if k < 3:
                @pl.when(jnp.logical_and(source(k, step), more))
                def _(i=i, step=step):
                    pass_att(k, step, 2 * k + i).start()

    def add(k, first=False):
        rows = pl.ds(pl.multiple_of(k * COLS, COLS), COLS)
        value = jnp.dot(gath[k], w_v[rows, :], preferred_element_type=F32)
        acc[...] = value if first else acc[...] + value

    locals_[3].wait()
    add(row(0), first=True)

    p2[0].wait_recv()
    p4.start()
    p3[0].start()
    m2[1].wait_recv()
    m4.start()
    m3[1].start()
    p2[1].wait_recv()
    p3[1].start()
    besides[-2].start()
    m2[0].wait_recv()
    m3[0].start()
    besides[2].start()
    send_quarter(1)
    send_quarter(3)
    p1.wait_recv()
    besides[-1].start()
    m1.wait_recv()
    besides[1].start()

    for p in (1, 2, 3):
        @pl.when(jnp.logical_and(x == p, crosses))
        def _(p=p):
            to_plane(p).wait_recv()
            from_plane(p).start()

    for j in (-2, 2, -1, 1):
        add(row(j))

    def other(j):
        besides[j].wait_recv()
        add(row(j, 1 - c))

    for j in (0, -2, 2, -1, 1):
        other(j)
    relay_att(1)

    for q in p3:
        q.wait_recv()
    besides[-3].start()
    add(row(-3))
    for q in m3:
        q.wait_recv()
    besides[3].start()
    add(row(3))
    p4.wait_recv()
    m4.wait_recv()
    besides[4].start()
    send_quarter(2)
    add(row(4))
    for j in (-3, 3, 4):
        other(j)

    d_own[...] = acc[...].astype(BF16)
    near, far = pl.ds(0, NEAR), pl.ds(NEAR, SEQ - NEAR)
    late = [remote(d_own.at[r], d_up.at[r], l_s.at[i], l_r.at[i], below) for i, r in enumerate((near, far))]
    hop = remote(d_own.at[far], relay2, l_s.at[1], l_r.at[2], (base + 3, t, d))
    hop_on = remote(relay2, d_up.at[far], l_s.at[2], l_r.at[1], (base - 1, t, d))

    @pl.when(x > 0)
    def _():
        late[0].start()
        late[1].start()

    @pl.when(jnp.logical_and(x == 0, crosses))
    def _():
        hop.start()
        late[0].start()

    mine = [pltpu.make_async_copy(gath.at[4 * d + i], gd.at[i, d], loc.at[4 + i]) for i in range(4)]
    for copy in mine:
        copy.start()

    has_above = s < 15

    def softmax_above():
        pos_copy.wait_recv()
        for h in range(NH):
            p_up[h] = probs_t(qkv_u, pos_u, h)

    def backward_above():
        for copy in late:
            copy.wait_recv()
        scale = 1.0 / math.sqrt(DH)
        for h in range(NH):
            p = p_up[h]
            da = d_up[:, h * DH:(h + 1) * DH]
            dp = dot(qkv_u[2 * NH + h], da, 1, 1)
            ds = (p * (dp - jnp.sum(p * dp, axis=0, keepdims=True))).astype(BF16)
            up_out[2 * NH + h] = dot(p.astype(BF16), da, 1, 0).astype(BF16)
            up_out[NH + h] = (dot(ds, qkv_u[h], 1, 0) * scale).astype(BF16)
            up_out[h] = (dot(ds, qkv_u[NH + h], 0, 0) * scale).astype(BF16)

    @pl.when(x < 3)
    def _():
        early.wait_recv()
        softmax_above()

    @pl.when(jnp.logical_and(x == 3, crosses))
    def _():
        hop.wait_recv()
        hop_on.start()

    relay_att(2)

    turn = 1 - 2 * (y % 2)
    pair, outer = row(turn), row(-turn)
    tt2 = 2 * (1 - y % 2) + c
    others = (d + 1 - 2 * (d % 2), 2 - d // 2, 3 - 3 * (d // 2))
    whole = pl.ds(0, SEQ)

    def swap(tile):
        cuts = ((0, whole, pair), (1, whole, outer), (2, lo, pair), (2, up, outer))
        return [
            remote(gd.at[tile, others[i], rows], gd.at[tile, others[i], rows], x_s.at[n], x_r.at[n], (s, dev, d))
            for n, (i, rows, dev) in enumerate(cuts)
        ]

    def across(tile, n):
        return [
            remote(gd.at[tile, r], gd.at[tile, r], x_s.at[n + i], x_r.at[n + i], (s, sib, d))
            for i, r in enumerate(others)
        ]

    there, missing, side1, side2 = swap(tt), swap(tt2), across(tt, 4), across(tt2, 8)
    sent_on = ((0,), (1,), (2, 3))
    for i, r in enumerate(others):
        remote(gath.at[0], gd.at[tt, r], z_s.at[0], z_r.at[r], (s, t, r)).wait_recv()
        for n in sent_on[i]:
            there[n].start()
        side1[i].start()

    @pl.when(x < 3)
    def _():
        backward_above()

    for i, r in enumerate(others):
        for n in sent_on[i]:
            missing[n].wait_recv()
        side2[i].start()

    for copy in mine:
        copy.wait()
    relay_att(3)
    for copy in side1 + side2:
        copy.wait_recv()
    rows = att[...].reshape(4 * SEQ, COLS)
    for i in range(4):
        dw_out[i * COLS:(i + 1) * COLS, :] = dot(gd[i].reshape(4 * SEQ, COLS), rows, 0, 0).astype(BF16)

    @pl.when(jnp.logical_and(x == 3, has_above))
    def _():
        cross.wait_recv()
        for p in (1, 2, 3):
            from_plane(p).wait_recv()
        softmax_above()
        backward_above()

    @pl.when(jnp.logical_not(has_above))
    def _():
        up_out[...] = jnp.zeros_like(up_out)

    for copy in p2 + m2 + [p1, m1] + p3 + m3 + [p4, m4] + list(besides.values()):
        copy.wait_send()
    for copy in there + side1 + side2:
        copy.wait_send()
    for m in range(4):
        away, copy = quarter(m)

        @pl.when(away)
        def _(copy=copy):
            copy.wait_send()

    for k in range(3):
        for i, (step, more) in enumerate(lines):
            @pl.when(jnp.logical_and(source(k, step), more))
            def _(k=k, i=i, step=step):
                pass_att(k, step, 2 * k + i).wait_send()

    @pl.when(x > 0)
    def _():
        early.wait_send()
        pos_copy.wait_send()
        late[0].wait_send()
        late[1].wait_send()

    @pl.when(jnp.logical_and(x == 0, crosses))
    def _():
        for p in (1, 2, 3):
            to_plane(p).wait_send()
        cross.wait_send()
        remote(pos_o, pos_u, e_s.at[6], e_r.at[1], below).wait_send()
        hop.wait_send()
        late[0].wait_send()

    for p in (1, 2, 3):
        @pl.when(jnp.logical_and(x == p, crosses))
        def _(p=p):
            from_plane(p).wait_send()

    @pl.when(jnp.logical_and(x == 3, crosses))
    def _():
        hop_on.wait_send()


def local(saved_qkv, positions, w_out, grad_out):
    qkv = jnp.transpose(saved_qkv[0, 0], (0, 2, 1, 3)).reshape(3 * NH, SEQ, DH)
    sems = pltpu.SemaphoreType.DMA
    any_, vmem = pl.BlockSpec(memory_space=pl.ANY), pl.BlockSpec(memory_space=pltpu.VMEM)
    dw, up = pl.pallas_call(
        kernel,
        out_shape=(
            jax.ShapeDtypeStruct((4 * COLS, COLS), BF16),
            jax.ShapeDtypeStruct((3 * NH, SEQ, DH), BF16),
        ),
        in_specs=[any_] * 4,
        out_specs=(vmem, vmem),
        scratch_shapes=[
            pltpu.VMEM((16, SEQ, COLS), BF16),
            pltpu.VMEM((16 * COLS, COLS), BF16),
            pltpu.VMEM((3 * NH, SEQ, DH), BF16),
            pltpu.VMEM((1, SEQ), jnp.int32),
            pltpu.VMEM((3 * NH, SEQ, DH), BF16),
            pltpu.VMEM((1, SEQ), jnp.int32),
            pltpu.VMEM((3, SEQ, DH), BF16),
            pltpu.VMEM((SEQ - NEAR, COLS), BF16),
            pltpu.VMEM((4, SEQ, COLS), BF16),
            pltpu.VMEM((4, 4, SEQ, COLS), BF16),
            pltpu.VMEM((SEQ, COLS), F32),
            pltpu.VMEM((SEQ, COLS), BF16),
            pltpu.VMEM((SEQ, COLS), BF16),
            pltpu.VMEM((NH, SEQ, SEQ), F32),
            sems((8,)), sems((12,)), sems((12,)), sems((8,)), sems((8,)), sems((4,)), sems((4,)),
            sems((6,)), sems((4,)), sems((7,)), sems((6,)), sems((3,)), sems((3,)), sems((12,)), sems((12,)),
        ],
        compiler_params=pltpu.CompilerParams(
            collective_id=0, has_side_effects=True, vmem_limit_bytes=VMEM_LIMIT
        ),
        cost_estimate=pl.CostEstimate(flops=1_300_000_000, bytes_accessed=7_000_000, transcendentals=100_000),
    )(*(pltpu.with_memory_space_constraint(a, pltpu.HBM) for a in (qkv, positions[0], w_out[0], grad_out[0, 0])))
    up = jnp.transpose(up.reshape(3, NH, SEQ, DH), (0, 2, 1, 3))
    return dw[None], up[None, None]


def solution(mesh):
    in_specs = (
        P("section", "dp", None, None, "st", None),
        P("section", "dp", None),
        P("section", None, "st"),
        P("section", "dp", None, "st"),
    )
    out_specs = (P("section", "dp", "st"), P("section", "dp", None, None, "st", None))
    return jax.shard_map(local, mesh=mesh, in_specs=in_specs, out_specs=out_specs, check_vma=False)
```
